32 devices in a mesh: frame: 8 (over z, x), patch: 4 (over y, core).
Axes of the slice: x: 2, y: 2, z: 4, core: 2. Of those that a mesh axis runs over, the one named last changes fastest.
Arguments:
- coeffs: float32 [16, 4, 8, 36], P('patch', None, 'frame'), may hold values from -1.8 to 1.8
- shifts: int32 [16, 4, 8, 2], P('patch', None, 'frame'), may hold values from -4 to 4
- pixels: bfloat16 [16, 4, 8, 128, 128], P('patch', None, 'frame'), may hold values from -6 to 6
- pupil_mask: int32 [64, 64], replicated, may hold values from 0 to 1, as said below
- chan_map: int32 [16], replicated, may hold values from 0 to 1, as said below
- intersection: int32 [4, 8], P('patch', 'frame'), may hold values from 4 to 16
Outputs:
- blended: float32 [2, 384, 768], P(None, 'patch', 'frame')
- coeff_grad: float32 [16, 4, 8, 36], P('patch', None, 'frame')
The draws below stay inside these ranges and needn't reach their ends.
Inputs may be any that keep to these rules, and one draw needn't show every extreme that they name: pupil_mask is 1 exactly on the cells whose centres lie in the disc of diameter 64 about the grid's centre, outside a central disc whose radius in cells is drawn from 8 to 21, and off one row and one column of cells (support vanes) whose positions are drawn from 0 to 63. `chan_map`: every channel is named by exactly 8 slots.
All inputs are finite; a program needn't handle non-finite values.
Results may differ from the reference program's by a relative error of at most 0.0003.
Values may be sent and summed in bfloat16 or wider, within the bound.
A program may use at most 64 MiB of HBM per device.

```python
import math
import jax
import jax.numpy as jnp
from jax import lax

N = 128
ZERN = 36
FRAMES = 8
CHANNELS = 2
MARGIN = 16
PUP = 64
TILE = 96
FC = 16
ROWS = 4
COLS = 8


def draw_pupil_mask(key, part):
    hole_radius = jax.random.randint(jax.random.fold_in(key, 11), (), PUP // 8, PUP // 3 + 1)
    vane_row = jax.random.randint(jax.random.fold_in(key, 13), (), 0, PUP)
    vane_col = jax.random.randint(jax.random.fold_in(key, 17), (), 0, PUP)
    counter = jnp.arange(PUP, dtype=jnp.int32)
    doubled = 2 * counter - (PUP - 1)
    radius_sq = doubled[:, None] * doubled[:, None] + doubled[None, :] * doubled[None, :]
    inside = (radius_sq <= PUP * PUP) & (radius_sq >= 4 * hole_radius * hole_radius)
    inside = inside & (counter[:, None] != vane_row) & (counter[None, :] != vane_col)
    return inside.astype(jnp.int32)


def draw_chan_map(key, part):
    shuffled = jax.random.permutation(jax.random.fold_in(key, 5), FC)
    return (shuffled // FRAMES).astype(jnp.int32)


def touch_ends(array, rng, smallest, top_value):
    shape = array.shape
    spot = [jax.random.randint(jax.random.fold_in(rng, axis), (), 0, shape[axis]) for axis in range(len(shape))]
    array = array.at[tuple(spot)].set(smallest)
    longest = shape.index(max(shape))
    spot[longest] = (spot[longest] + 1) % shape[longest]
    return array.at[tuple(spot)].set(top_value)


def block_scale(stream_key, dims, split, smallest, largest):
    def one(dim, shards_of):
        draws = jax.random.uniform(jax.random.fold_in(jax.random.fold_in(stream_key, 6), dim), (shards_of,), jnp.float32, smallest / len(split), largest / len(split))
        return jnp.repeat(jnp.exp(draws), dims[dim] // shards_of).reshape((-1,) + (1,) * (len(dims) - dim - 1))

    factor_of = one(*split[0])
    for cut in split[1:]:
        factor_of = factor_of * one(*cut)
    return factor_of


def noise(own_key, dims, deviation, reach, pieces=(), kind=jnp.bfloat16):
    loudness = block_scale(own_key, dims, pieces, -0.22, 0.18) if pieces else 1.0
    array = jax.random.normal(own_key, dims, jnp.float32) * deviation * loudness
    return jnp.minimum(jnp.maximum(array, -reach), reach).astype(kind)


def setup_inputs(seed: int = 0) -> dict:
    streams_of = jax.random.split(jax.random.key(seed), 7)
    return {
        "coeffs": noise(streams_of[0], (FC, ROWS, COLS, ZERN), 0.3, 1.8, ((0, 4), (2, 8)), jnp.float32),
        "shifts": touch_ends(jax.random.randint(streams_of[1], (FC, ROWS, COLS, 2), -4, 5), jax.random.fold_in(streams_of[1], 1), -4, 4).astype(jnp.int32),
        "pixels": noise(streams_of[2], (FC, ROWS, COLS, N, N), 1.0, 6.0, ((0, 4), (2, 8))),
        "pupil_mask": draw_pupil_mask(jax.random.fold_in(streams_of[6], 71), 0),
        "chan_map": draw_chan_map(jax.random.fold_in(streams_of[6], 71), 0),
        "intersection": touch_ends(jax.random.randint(streams_of[5], (ROWS, COLS), MARGIN // 4, MARGIN + 1), jax.random.fold_in(streams_of[5], 1), MARGIN // 4, MARGIN).astype(jnp.int32),
    }


highest = lax.Precision.HIGHEST
regular_gamma = 0.1
wave_ratio = 0.35

def product(form, left, right):
    return jnp.einsum(form, left, right, precision=highest)

def noll_order(noll_index):
    radial = 0
    remain = noll_index - 1
    while remain > radial:
        radial += 1
        remain -= radial
    azimuth = radial % 2 + 2 * ((remain + (radial + 1) % 2) // 2)
    if noll_index % 2 == 1:
        azimuth = -azimuth
    return (radial, azimuth)

def zernike_basis(mode_count, pupil_side):
    position = (jnp.arange(pupil_side, dtype=jnp.int32).astype(jnp.float32) - (pupil_side - 1) / 2.0) / (pupil_side / 2.0)
    grid_y = position[:, None] + jnp.zeros((1, pupil_side), jnp.float32)
    grid_x = jnp.zeros((pupil_side, 1), jnp.float32) + position[None, :]
    radius = jnp.sqrt(grid_x * grid_x + grid_y * grid_y)
    angle_map = jnp.arctan2(grid_y, grid_x)
    collected = []
    for noll_index in range(2, mode_count + 2):
        radial, azimuth = noll_order(noll_index)
        order_abs = abs(azimuth)
        radial_sum = jnp.zeros_like(radius)
        for power_step in range((radial - order_abs) // 2 + 1):
            factor = math.factorial(radial - power_step) / (math.factorial(power_step) * math.factorial((radial + order_abs) // 2 - power_step) * math.factorial((radial - order_abs) // 2 - power_step))
            if power_step % 2 == 1:
                factor = -factor
            radial_sum = radial_sum + factor * radius ** (radial - 2 * power_step)
        if azimuth == 0:
            shaped = radial_sum * math.sqrt(radial + 1.0)
        elif azimuth > 0:
            shaped = radial_sum * math.sqrt(2.0 * (radial + 1.0)) * jnp.cos(order_abs * angle_map)
        else:
            shaped = radial_sum * math.sqrt(2.0 * (radial + 1.0)) * jnp.sin(order_abs * angle_map)
        collected.append(shaped.reshape(-1))
    return jnp.stack(collected)

def dft_tables(length, width):
    frequency = jnp.arange(length, dtype=jnp.int32)[:, None]
    position = jnp.arange(width, dtype=jnp.int32)[None, :]
    turns = (frequency * position % length).astype(jnp.float32) * (2.0 * math.pi / length)
    return (jnp.cos(turns), -jnp.sin(turns))

def real_transform(image, length):
    full_re, full_im = dft_tables(length, length)
    inner_re = product('bxy,vy->bxv', image, full_re)
    inner_im = product('bxy,vy->bxv', image, full_im)
    out_re = product('ux,bxv->buv', full_re, inner_re) - product('ux,bxv->buv', full_im, inner_im)
    out_im = product('ux,bxv->buv', full_re, inner_im) + product('ux,bxv->buv', full_im, inner_re)
    return (out_re, out_im)

def build_otf(coeff_in, scale_in, shift_in, zernike, mask_flat, length):
    pupil_side = length // 2
    batch_size = coeff_in.shape[0]
    phase_map = jnp.dot(coeff_in, zernike, precision=highest) * scale_in[:, None]
    pupil_re = (mask_flat * jnp.cos(phase_map)).reshape(batch_size, pupil_side, pupil_side)
    pupil_im = (mask_flat * jnp.sin(phase_map)).reshape(batch_size, pupil_side, pupil_side)
    left_re, left_im = dft_tables(length, pupil_side)
    half_re = product('bxy,vy->bxv', pupil_re, left_re) - product('bxy,vy->bxv', pupil_im, left_im)
    half_im = product('bxy,vy->bxv', pupil_re, left_im) + product('bxy,vy->bxv', pupil_im, left_re)
    field_re = product('ux,bxv->buv', left_re, half_re) - product('ux,bxv->buv', left_im, half_im)
    field_im = product('ux,bxv->buv', left_re, half_im) + product('ux,bxv->buv', left_im, half_re)
    intensity = field_re * field_re + field_im * field_im
    point_spread = intensity / lax.optimization_barrier(jnp.sum(intensity, axis=(1, 2), keepdims=True))
    otf_re, otf_im = real_transform(point_spread, length)
    frequency = jnp.arange(length, dtype=jnp.int32).astype(jnp.float32)
    angle_y = 2.0 * math.pi / length * shift_in[:, 0:1] * frequency[None, :]
    angle_x = 2.0 * math.pi / length * shift_in[:, 1:2] * frequency[None, :]
    total_angle = angle_y[:, :, None] + angle_x[:, None, :]
    tilt_re = jnp.cos(total_angle)
    tilt_im = -jnp.sin(total_angle)
    return (otf_re * tilt_re - otf_im * tilt_im, otf_re * tilt_im + otf_im * tilt_re)

def data_spectrum(pixel_in, length, margin):
    position = jnp.arange(length, dtype=jnp.int32)
    distance = jnp.minimum(position, length - 1 - position).astype(jnp.float32)
    taper_row = jnp.where(distance < margin, 0.5 - 0.5 * jnp.cos(math.pi * (distance + 0.5) / margin), 1.0)
    image = pixel_in.astype(jnp.float32) * taper_row[:, None] * taper_row[None, :]
    return real_transform(image, length)

def wiener_object(otf_re, otf_im, spec_re, spec_im, onehot):
    cross_re = otf_re * spec_re + otf_im * spec_im
    cross_im = otf_re * spec_im - otf_im * spec_re
    intensity = otf_re * otf_re + otf_im * otf_im
    num_re = product('kc,kbuv->cbuv', onehot, cross_re)
    num_im = product('kc,kbuv->cbuv', onehot, cross_im)
    denominator = product('kc,kbuv->cbuv', onehot, intensity) + regular_gamma
    return (num_re / denominator, num_im / denominator)

def object_image(obj_re, obj_im, length):
    full_re, full_im = dft_tables(length, length)
    back_re = product('ux,bxv->buv', full_re, obj_re) + product('ux,bxv->buv', full_im, obj_im)
    back_im = product('ux,bxv->buv', full_re, obj_im) - product('ux,bxv->buv', full_im, obj_re)
    return (product('bux,vx->buv', back_re, full_re) + product('bux,vx->buv', back_im, full_im)) / (length * length)

def window_weight(width_in, length):
    position = jnp.arange(length, dtype=jnp.int32)
    distance = (jnp.minimum(position, length - 1 - position) + 1).astype(jnp.float32)
    ramp_row = jnp.minimum(1.0, distance / (width_in.astype(jnp.float32) + 1.0))
    return ramp_row[:, None] * ramp_row[None, :]

def reference(coeffs, shifts, pixels, pupil_mask, chan_map, intersection):
    length = N
    zernike = zernike_basis(ZERN, PUP)
    mask_flat = pupil_mask.reshape(-1).astype(jnp.float32)
    scale_all = 1.0 / (1.0 + wave_ratio * chan_map.astype(jnp.float32))
    onehot = (chan_map[:, None] == jnp.arange(CHANNELS, dtype=jnp.int32)[None, :]).astype(jnp.float32)
    patch_count = ROWS * COLS
    coeff_patch = jnp.transpose(coeffs, (1, 2, 0, 3)).reshape(patch_count, FC, ZERN)
    shift_patch = jnp.transpose(shifts, (1, 2, 0, 3)).reshape(patch_count, FC, 2).astype(jnp.float32)
    pixel_patch = jnp.transpose(pixels, (1, 2, 0, 3, 4)).reshape(patch_count, FC, N, N)
    width_patch = intersection.reshape(patch_count)
    loss_scale = 1.0 / float(length * length * length)

    def one_patch(packed):
        coeff_one, shift_one, pixel_one, width_one = packed
        spec_re, spec_im = data_spectrum(pixel_one, length, MARGIN)
        spec_re = spec_re[:, None]
        spec_im = spec_im[:, None]

        def metric(coeff_in):
            otf_re, otf_im = build_otf(coeff_in, scale_all, shift_one, zernike, mask_flat, length)
            otf_re = otf_re[:, None]
            otf_im = otf_im[:, None]
            obj_re, obj_im = wiener_object(otf_re, otf_im, spec_re, spec_im, onehot)
            obj_re = lax.stop_gradient(obj_re)
            obj_im = lax.stop_gradient(obj_im)
            per_re = product('kc,cbuv->kbuv', onehot, obj_re)
            per_im = product('kc,cbuv->kbuv', onehot, obj_im)
            res_re = spec_re - (per_re * otf_re - per_im * otf_im)
            res_im = spec_im - (per_re * otf_im + per_im * otf_re)
            total = jnp.sum(res_re * res_re + res_im * res_im) + regular_gamma * jnp.sum(obj_re * obj_re + obj_im * obj_im)
            return (total * loss_scale, (obj_re, obj_im))
        grad_one, objects = jax.grad(metric, has_aux=True)(coeff_one)
        image = object_image(objects[0][:, 0], objects[1][:, 0], length)
        weight = window_weight(width_one, length)
        stacked = jnp.concatenate([image * weight[None], weight[None]], axis=0)
        return (grad_one, stacked)
    grads, windows = lax.map(one_patch, (coeff_patch, shift_patch, pixel_patch, width_patch))
    height = ROWS * TILE + 2 * MARGIN
    breadth = COLS * TILE + 2 * MARGIN
    canvas = jnp.zeros((CHANNELS + 1, height, breadth), jnp.float32)

    def place(counter, canvas_in):
        row_at = (counter // COLS * TILE).astype(jnp.int32)
        col_at = (counter % COLS * TILE).astype(jnp.int32)
        start = (jnp.zeros((), jnp.int32), row_at, col_at)
        current = lax.dynamic_slice(canvas_in, start, (CHANNELS + 1, N, N))
        return lax.dynamic_update_slice(canvas_in, current + windows[counter], start)
    canvas = lax.fori_loop(0, patch_count, place, canvas)
    inner = canvas[:, MARGIN:MARGIN + ROWS * TILE, MARGIN:MARGIN + COLS * TILE]
    blended = inner[:CHANNELS] / inner[CHANNELS][None]
    coeff_grad = jnp.transpose(grads.reshape(ROWS, COLS, FC, ZERN), (2, 0, 1, 3))
    return (blended, coeff_grad)
```

```python
import functools
import math

import jax
import jax.numpy as jnp
import ml_dtypes
import numpy as np
from jax import lax
from jax.experimental import pallas as pl
from jax.experimental.pallas import tpu as pltpu
from jax.sharding import PartitionSpec as P

CHANNELS = 2
MARGIN = 16
GAMMA = 0.1
RATIO = 0.35

f32 = jnp.float32
bf16 = jnp.bfloat16


def noll_order(noll_index):
    radial = 0
    remain = noll_index - 1
    while remain > radial:
        radial += 1
        remain -= radial
    azimuth = radial % 2 + 2 * ((remain + (radial + 1) % 2) // 2)
    if noll_index % 2 == 1:
        azimuth = -azimuth
    return (radial, azimuth)


def zernike_basis(mode_count, side):
    pos = (np.arange(side) - (side - 1) / 2.0) / (side / 2.0)
    grid_y = pos[:, None] + np.zeros((1, side))
    grid_x = np.zeros((side, 1)) + pos[None, :]
    radius = np.sqrt(grid_x**2 + grid_y**2)
    angle = np.arctan2(grid_y, grid_x)
    out = []
    for noll_index in range(2, mode_count + 2):
        radial, azimuth = noll_order(noll_index)
        m = abs(azimuth)
        total = np.zeros_like(radius)
        for k in range((radial - m) // 2 + 1):
            factor = math.factorial(radial - k) / (
                math.factorial(k)
                * math.factorial((radial + m) // 2 - k)
                * math.factorial((radial - m) // 2 - k)
            )
            total = total + (-1) ** k * factor * radius ** (radial - 2 * k)
        if azimuth == 0:
            out.append(total * math.sqrt(radial + 1.0))
        elif azimuth > 0:
            out.append(total * math.sqrt(2.0 * (radial + 1.0)) * np.cos(m * angle))
        else:
            out.append(total * math.sqrt(2.0 * (radial + 1.0)) * np.sin(m * angle))
    return np.stack(out)


def np_split(table):
    high = table.astype(np.float32).astype(ml_dtypes.bfloat16)
    low = (table - high.astype(np.float64)).astype(np.float32).astype(ml_dtypes.bfloat16)
    return high, low


def left_form(a):
    return np.block([[a.real, -a.imag], [a.imag, a.real]])


def right_form(a):
    return np.block([[a.real, a.imag], [-a.imag, a.real]])


def half_rows(n):
    return -(-(n // 2 + 1) // 8) * 8


def make_tables(n, margin):
    side = n // 2
    rows = half_rows(n)
    index = np.arange(n)
    full = np.exp(-2j * np.pi * ((index[:, None] * index[None, :]) % n) / n)
    part = full[:, :side]
    dist = np.minimum(index, n - 1 - index)
    taper = np.where(dist < margin, 0.5 - 0.5 * np.cos(np.pi * (dist + 0.5) / margin), 1.0)
    valid = np.arange(rows) <= n // 2
    half = np.where(valid[:, None], full[np.arange(rows) % n], 0.0)
    double = np.where(valid, np.where(np.arange(rows) % (n // 2) == 0, 1.0, 2.0), 0.0)
    tables = {}
    h, l = np_split(right_form(part.T))
    tables["t1a"], tables["t1l"] = np.concatenate([h, h]), l
    h, l = np_split(left_form(part))
    tables["t2a"], tables["t2l"] = np.concatenate([h, h], 1), l
    real_right = np.concatenate([full.T.real, full.T.imag], 1)
    h, l = np_split(real_right)
    tables["taa"], tables["tal"] = np.concatenate([h, h]), l
    h, l = np_split(real_right * taper[:, None])
    tables["tpa"] = np.concatenate([h, l])
    h, l = np_split(left_form(half))
    tables["tb"] = np.concatenate([h, l])
    h, l = np_split(left_form(half * taper[None, :]))
    tables["tbp"] = np.concatenate([h, l])
    h, l = np_split(left_form(half.conj().T * double[None, :]))
    tables["ub"] = np.concatenate([h, l])
    h, l = np_split(np.concatenate([full.real, full.imag]))
    tables["ua"] = np.concatenate([h, l], 1)
    h, l = np_split(left_form(part.conj().T))
    tables["u2"] = np.concatenate([h, l])
    h, l = np_split(right_form(part.conj()))
    tables["u1"] = np.concatenate([h, l], 1)
    return tables


NAMES = ("t1a", "t1l", "t2a", "t2l", "taa", "tal", "tpa", "tb", "tbp", "ub", "ua", "u2", "u1")


def split(x):
    high = x.astype(bf16)
    return high, (x - high.astype(f32)).astype(bf16)


def dot(a, b):
    return jnp.dot(a, b, preferred_element_type=f32)


def rows_cat(*parts):
    return jnp.concatenate(parts, axis=0)


def lanes_cat(*parts):
    return jnp.concatenate(parts, axis=1)


def left_wide(table, high, low):
    m = table.shape[0] // 2
    both = dot(table, high)
    return both[:m] + both[m:] + dot(table[:m], low)


def right_wide(x, table):
    m = table.shape[1] // 2
    high, low = split(x)
    both = dot(high, table)
    return both[:, :m] + both[:, m:] + dot(low, table[:, :m])


def sincos_small(r):
    z = r * r
    s = r + r * z * (-1.6666654611e-1 + z * (8.3321608736e-3 + z * -1.9515295891e-4))
    c = 1.0 - 0.5 * z + z * z * (4.166664568298827e-2 + z * (-1.388731625493765e-3 + z * 2.443315711809948e-5))
    return s, c


def quadrant(s, c, q):
    swap = (q & 1) == 1
    sn = jnp.where(swap, c, s)
    cs = jnp.where(swap, s, c)
    sn = jnp.where((q & 2) == 2, -sn, sn)
    cs = jnp.where(((q + 1) & 2) == 2, -cs, cs)
    return sn, cs


def sincos(x, turn):
    k = jnp.round(x * (2.0 / math.pi))
    r = x - k * 1.5703125
    r = r - k * 4.837512969970703125e-4
    r = r - k * 7.549789948768648e-8
    s, c = sincos_small(r)
    return quadrant(s, c, k.astype(jnp.int32) + turn)


def paired(x, r):
    n = x.shape[1] // 2
    return rows_cat(
        lanes_cat(x[:r, :n], x[r:, :n]), lanes_cat(x[:r, n:], x[r:, n:])
    )


def unpaired(x, r):
    n = x.shape[1] // 2
    return rows_cat(
        lanes_cat(x[:r, :n], x[r:, :n]), lanes_cat(x[:r, n:], x[r:, n:])
    )


def forward_pairs(base, pairs, n, modes, coef, chan, zern, mask, t, q_s, f_s, h_s, inv_s):
    side = n // 2
    hr = half_rows(n)
    count = 2 * pairs
    acc = [jnp.zeros((side, n), f32) for _ in range(count)]
    for j in range(modes):
        z = zern[j]
        for g in range(count):
            acc[g] = acc[g] + coef[base + g, j] * z
    turn = jnp.where(lax.broadcasted_iota(jnp.int32, (side, n), 1) < side, 1, 0)
    pupils = []
    for g in range(count):
        scale = 1.0 / (1.0 + RATIO * jnp.full((1, n), chan[base + g], jnp.int32).astype(f32))
        sn, cs = sincos(acc[g] * scale, turn)
        pupils.append(mask * sn)
        q_s[base + g] = mask * cs * scale
    for p in range(pairs):
        s0 = base + 2 * p
        high, low = split(rows_cat(pupils[2 * p], pupils[2 * p + 1]))
        half = dot(lanes_cat(high, low), t["t1a"][...]) + dot(high, t["t1l"][...])
        high, low = split(paired(half, side))
        field = dot(t["t2a"][...], rows_cat(high, low)) + dot(t["t2l"][...], high)
        f_s[s0] = field[:, :n]
        f_s[s0 + 1] = field[:, n:]
        inten = field[:n] * field[:n] + field[n:] * field[n:]
        inv0 = 1.0 / jnp.sum(inten[:, :n], keepdims=True)
        inv1 = 1.0 / jnp.sum(inten[:, n:], keepdims=True)
        inv_s[s0] = jnp.broadcast_to(inv0, (8, n))
        inv_s[s0 + 1] = jnp.broadcast_to(inv1, (8, n))
        high, low = split(rows_cat(inten[:, :n], inten[:, n:]))
        inner = dot(lanes_cat(high, low), t["taa"][...]) + dot(high, t["tal"][...])
        high, low = split(paired(inner, n))
        otf = left_wide(t["tb"][...], high, low)
        h_s[s0] = otf[:, :n] * inv0
        h_s[s0 + 1] = otf[:, n:] * inv1


def spectrum_pairs(base, pairs, n, pix, shift, chan, t, h_s, s_s, num_s, den_s):
    hr = half_rows(n)
    row = lax.broadcasted_iota(jnp.int32, (hr, n), 0)
    col = lax.broadcasted_iota(jnp.int32, (hr, n), 1)
    num = [[num_s[c, :hr], num_s[c, hr:]] for c in range(CHANNELS)]
    den = [den_s[c] for c in range(CHANNELS)]
    for p in range(pairs):
        s0 = base + 2 * p
        both = rows_cat(pix[s0], pix[s0 + 1])
        inner = dot(lanes_cat(both, both), t["tpa"][...])
        high, low = split(paired(inner, n))
        spec = left_wide(t["tbp"][...], high, low)
        for g in range(2):
            s = s0 + g
            sr = spec[:hr, g * n : (g + 1) * n]
            si = spec[hr:, g * n : (g + 1) * n]
            turns = (row * shift[s, 0] + col * shift[s, 1]) & (n - 1)
            quarter = n // 4
            q = (turns + quarter // 2) // quarter
            rest = (turns - q * quarter).astype(f32) * (2.0 * math.pi / n)
            sn, cs = quadrant(*sincos_small(rest), q)
            vr = sr * cs - si * sn
            vi = sr * sn + si * cs
            s_s[s, :hr] = vr
            s_s[s, hr:] = vi
            hre = h_s[s, :hr]
            him = h_s[s, hr:]
            cr = hre * vr + him * vi
            ci = hre * vi - him * vr
            power = hre * hre + him * him
            for c in range(CHANNELS):
                mine = jnp.full((1, n), chan[s], jnp.int32) == c
                num[c][0] = num[c][0] + jnp.where(mine, cr, 0.0)
                num[c][1] = num[c][1] + jnp.where(mine, ci, 0.0)
                den[c] = den[c] + jnp.where(mine, power, 0.0)
    for c in range(CHANNELS):
        num_s[c, :hr] = num[c][0]
        num_s[c, hr:] = num[c][1]
        den_s[c] = den[c]


def back_transform(left, right, n, t):
    high, low = split(lanes_cat(left, right))
    part = left_wide(t["ub"][...], high, low)
    return right_wide(unpaired(part, n), t["ua"][...])


def backward_pairs(base, pairs, n, modes, chan, zern, t, q_s, f_s, h_s, inv_s, s_s, obj_s, cg_s):
    side = n // 2
    hr = half_rows(n)
    loss = 1.0 / float(n * n * n)
    weights = []
    for p in range(pairs):
        s0 = base + 2 * p
        grads = []
        for g in range(2):
            s = s0 + g
            first = jnp.full((1, n), chan[s], jnp.int32) == 0
            o_re = jnp.where(first, obj_s[0, :hr], obj_s[1, :hr])
            o_im = jnp.where(first, obj_s[0, hr:], obj_s[1, hr:])
            hre = h_s[s, :hr]
            him = h_s[s, hr:]
            rre = s_s[s, :hr] - (o_re * hre - o_im * him)
            rim = s_s[s, hr:] - (o_re * him + o_im * hre)
            grads.append(
                rows_cat(
                    (-2.0 * loss) * (rre * o_re + rim * o_im),
                    (2.0 * loss) * (rre * o_im - rim * o_re),
                )
            )
        psf_grad = back_transform(grads[0], grads[1], n, t)
        field_grads = []
        for g in range(2):
            s = s0 + g
            pg = psf_grad[g * n : (g + 1) * n]
            fr = f_s[s, :n]
            fi = f_s[s, n:]
            inv = inv_s[s][:1]
            mean = inv * jnp.sum(pg * (fr * fr + fi * fi), keepdims=True)
            gi = (2.0 * inv) * (pg - mean)
            field_grads.append(rows_cat(fr * gi, fi * gi))
        high, low = split(lanes_cat(field_grads[0], field_grads[1]))
        part = left_wide(t["u2"][...], high, low)
        pupil_grad = right_wide(unpaired(part, side), t["u1"][...])
        for g in range(2):
            weights.append(q_s[s0 + g] * pupil_grad[g * side : (g + 1) * side])
    pad = cg_s.shape[1]
    for j in range(modes):
        z = zern[j]
        for g in range(2 * pairs):
            cg_s[base + g, j : j + 1] = jnp.sum(z * weights[g], axis=0, keepdims=True)


def window_weight(width, n):
    def ramp(axis):
        pos = lax.broadcasted_iota(jnp.int32, (n, n), axis)
        dist = (jnp.minimum(pos, n - 1 - pos) + 1).astype(f32)
        return jnp.minimum(1.0, dist / (jnp.full((1, n), width, jnp.int32).astype(f32) + 1.0))

    return ramp(0) * ramp(1)


def kernel(n, modes, slots, group, coef, shift, chan, inter, pix, mask_ref, zern, *rest):
    t = dict(zip(NAMES, rest[: len(NAMES)]))
    canvas, grad, q_s, f_s, h_s, inv_s, s_s, num_s, den_s, obj_s, cg_s = rest[len(NAMES) :]
    hr = half_rows(n)
    pairs = group // 2
    m = mask_ref[...].astype(f32)
    mask = lanes_cat(m, m)
    cg_s[...] = jnp.zeros_like(cg_s)
    num_s[...] = jnp.zeros_like(num_s)
    den_s[...] = jnp.zeros_like(den_s)

    @pl.loop(0, slots // group)
    def _(i):
        forward_pairs(i * group, pairs, n, modes, coef, chan, zern, mask, t, q_s, f_s, h_s, inv_s)

    @pl.loop(0, slots // group)
    def _(i):
        spectrum_pairs(i * group, pairs, n, pix, shift, chan, t, h_s, s_s, num_s, den_s)

    for c in range(CHANNELS):
        d = 1.0 / (den_s[c] + GAMMA)
        obj_s[c, :hr] = num_s[c, :hr] * d
        obj_s[c, hr:] = num_s[c, hr:] * d
    images = back_transform(obj_s[0], obj_s[1], n, t) * (1.0 / (n * n))
    weight = window_weight(inter[0, 0], n)
    canvas[0] = images[:n] * weight
    canvas[1] = images[n:] * weight
    canvas[2] = weight

    @pl.loop(0, slots // group)
    def _(i):
        backward_pairs(
            i * group, pairs, n, modes, chan, zern, t, q_s, f_s, h_s, inv_s, s_s, obj_s, cg_s
        )

    flat = cg_s[...].reshape(slots * cg_s.shape[1], n)
    grad[...] = lax.dot_general(
        jnp.ones((8, n), f32), flat, (((1,), (1,)), ((), ())),
        precision=lax.Precision.HIGHEST, preferred_element_type=f32,
    )


def padded(cells, sides, width):
    for axis, dim in sides:
        count = lax.axis_size(axis)
        ends = count - 1
        head = lax.slice_in_dim(cells, 0, width, axis=dim)
        tail = lax.slice_in_dim(cells, cells.shape[dim] - width, cells.shape[dim], axis=dim)
        cells = jnp.concatenate(
            [
                lax.ppermute(tail, axis, [(i, (i + 1) % count) for i in range(ends)]),
                cells,
                lax.ppermute(head, axis, [((i + 1) % count, i) for i in range(ends)]),
            ],
            axis=dim,
        )
    return cells


def fold_margins(extended, axis_num, margin):
    span = extended.shape[axis_num] - 4 * margin
    upper_part = lax.slice_in_dim(extended, 0, margin, axis=axis_num)
    middle = lax.slice_in_dim(extended, 2 * margin, 2 * margin + span, axis=axis_num)
    lower_part = lax.slice_in_dim(extended, span + 3 * margin, span + 4 * margin, axis=axis_num)
    pad_upper = [(0, 0)] * extended.ndim
    pad_lower = [(0, 0)] * extended.ndim
    pad_upper[axis_num] = (0, span - margin)
    pad_lower[axis_num] = (span - margin, 0)
    return middle + jnp.pad(upper_part, pad_upper) + jnp.pad(lower_part, pad_lower)


def per_device(coeffs, shifts, pixels, pupil_mask, chan_map, intersection):
    modes = coeffs.shape[3]
    n = pixels.shape[3]
    margin = MARGIN
    slots = chan_map.shape[0]
    group = 4
    hr = half_rows(n)
    side = n // 2
    pad = -(-modes // 8) * 8
    own_pix = lax.all_to_all(pixels, "patch", split_axis=1, concat_axis=0, tiled=True)
    both = jnp.concatenate([coeffs, shifts.astype(f32)], axis=3)
    both = lax.all_to_all(both, "patch", split_axis=1, concat_axis=0, tiled=True)
    both = both.reshape(slots, modes + 2)
    own_coef = both[:, :modes]
    own_shift = both[:, modes:].astype(jnp.int32)
    z = zernike_basis(modes, side)
    zern = jnp.asarray(np.concatenate([z, z], axis=2).astype(np.float32))
    tables = make_tables(n, margin)
    smem = pl.BlockSpec(memory_space=pltpu.SMEM)
    vmem = pl.BlockSpec(memory_space=pltpu.VMEM)
    canvas, grad = pl.pallas_call(
        functools.partial(kernel, n, modes, slots, group),
        out_shape=(
            jax.ShapeDtypeStruct((CHANNELS + 1, n, n), f32),
            jax.ShapeDtypeStruct((8, slots * pad), f32),
        ),
        in_specs=[smem] * 4 + [vmem] * (3 + len(NAMES)),
        out_specs=(vmem, vmem),
        scratch_shapes=[
            pltpu.VMEM((slots, side, n), f32),
            pltpu.VMEM((slots, 2 * n, n), f32),
            pltpu.VMEM((slots, 2 * hr, n), f32),
            pltpu.VMEM((slots, 8, n), f32),
            pltpu.VMEM((slots, 2 * hr, n), f32),
            pltpu.VMEM((CHANNELS, 2 * hr, n), f32),
            pltpu.VMEM((CHANNELS, hr, n), f32),
            pltpu.VMEM((CHANNELS, 2 * hr, n), f32),
            pltpu.VMEM((slots, pad, n), f32),
        ],
        compiler_params=pltpu.CompilerParams(vmem_limit_bytes=48 * 1024 * 1024),
    )(
        own_coef, own_shift, chan_map, intersection, own_pix.reshape(slots, n, n), pupil_mask, zern,
        *[jnp.asarray(tables[name]) for name in NAMES],
    )
    grad = grad[0].reshape(slots, pad)[:, :modes].reshape(slots, 1, 1, modes)
    coeff_grad = lax.all_to_all(grad, "patch", split_axis=0, concat_axis=1, tiled=True)
    extended = padded(canvas, (("frame", 2), ("patch", 1)), margin)
    folded = fold_margins(fold_margins(extended, 1, margin), 2, margin)
    blended = folded[:CHANNELS] / folded[CHANNELS][None]
    return (blended, coeff_grad)


def solution(mesh):
    in_specs = (
        P("patch", None, "frame", None),
        P("patch", None, "frame", None),
        P("patch", None, "frame", None, None),
        P(),
        P(),
        P("patch", "frame"),
    )
    out_specs = (P(None, "patch", "frame"), P("patch", None, "frame", None))
    return jax.shard_map(
        per_device, mesh=mesh, in_specs=in_specs, out_specs=out_specs, check_vma=False
    )
```

```python
import functools
import math

import jax
import jax.numpy as jnp
import ml_dtypes
import numpy as np
from jax import lax
from jax.experimental import pallas as pl
from jax.experimental.pallas import tpu as pltpu
from jax.sharding import PartitionSpec as P

CHANNELS = 2
MARGIN = 16
GAMMA = 0.1
RATIO = 0.35

f32 = jnp.float32
bf16 = jnp.bfloat16


def noll_order(noll_index):
    radial = 0
    remain = noll_index - 1
    while remain > radial:
        radial += 1
        remain -= radial
    azimuth = radial % 2 + 2 * ((remain + (radial + 1) % 2) // 2)
    if noll_index % 2 == 1:
        azimuth = -azimuth
    return (radial, azimuth)


def zernike_basis(mode_count, side):
    pos = (np.arange(side) - (side - 1) / 2.0) / (side / 2.0)
    grid_y = pos[:, None] + np.zeros((1, side))
    grid_x = np.zeros((side, 1)) + pos[None, :]
    radius = np.sqrt(grid_x**2 + grid_y**2)
    angle = np.arctan2(grid_y, grid_x)
    out = []
    for noll_index in range(2, mode_count + 2):
        radial, azimuth = noll_order(noll_index)
        m = abs(azimuth)
        total = np.zeros_like(radius)
        for k in range((radial - m) // 2 + 1):
            factor = math.factorial(radial - k) / (
                math.factorial(k)
                * math.factorial((radial + m) // 2 - k)
                * math.factorial((radial - m) // 2 - k)
            )
            total = total + (-1) ** k * factor * radius ** (radial - 2 * k)
        if azimuth == 0:
            out.append(total * math.sqrt(radial + 1.0))
        elif azimuth > 0:
            out.append(total * math.sqrt(2.0 * (radial + 1.0)) * np.cos(m * angle))
        else:
            out.append(total * math.sqrt(2.0 * (radial + 1.0)) * np.sin(m * angle))
    return np.stack(out)


def np_split(table):
    high = table.astype(np.float32).astype(ml_dtypes.bfloat16)
    low = (table - high.astype(np.float64)).astype(np.float32).astype(ml_dtypes.bfloat16)
    return high, low


def left_form(a):
    return np.block([[a.real, -a.imag], [a.imag, a.real]])


def right_form(a):
    return np.block([[a.real, a.imag], [-a.imag, a.real]])


def half_rows(n):
    return -(-(n // 2 + 1) // 8) * 8


def make_tables(n, margin):
    side = n // 2
    rows = half_rows(n)
    index = np.arange(n)
    full = np.exp(-2j * np.pi * ((index[:, None] * index[None, :]) % n) / n)
    part = full[:, :side]
    dist = np.minimum(index, n - 1 - index)
    taper = np.where(dist < margin, 0.5 - 0.5 * np.cos(np.pi * (dist + 0.5) / margin), 1.0)
    valid = np.arange(rows) <= n // 2
    half = np.where(valid[:, None], full[np.arange(rows) % n], 0.0)
    double = np.where(valid, np.where(np.arange(rows) % (n // 2) == 0, 1.0, 2.0), 0.0)
    tables = {}
    h, l = np_split(right_form(part.T))
    tables["t1a"], tables["t1l"] = np.concatenate([h, h]), l
    h, l = np_split(left_form(part))
    tables["t2a"], tables["t2l"] = np.concatenate([h, h], 1), l
    real_right = np.concatenate([full.T.real, full.T.imag], 1)
    h, l = np_split(real_right)
    tables["taa"], tables["tal"] = np.concatenate([h, h]), l
    h, l = np_split(real_right * taper[:, None])
    tables["tpa"] = np.concatenate([h, l])
    h, l = np_split(left_form(half))
    tables["tb"] = np.concatenate([h, l])
    h, l = np_split(left_form(half * taper[None, :]))
    tables["tbp"] = np.concatenate([h, l])
    h, l = np_split(left_form(half.conj().T * double[None, :]))
    tables["ub"] = np.concatenate([h, l])
    h, l = np_split(np.concatenate([full.real, full.imag]))
    tables["ua"] = np.concatenate([h, l], 1)
    h, l = np_split(left_form(part.conj().T))
    tables["u2"] = np.concatenate([h, l])
    h, l = np_split(right_form(part.conj()))
    tables["u1"] = np.concatenate([h, l], 1)
    return tables


NAMES = ("t1a", "t1l", "t2a", "t2l", "taa", "tal", "tpa", "tb", "tbp", "ub", "ua", "u2", "u1")
MESH = pl.DeviceIdType.MESH


def pack_tables(n, margin):
    tables = make_tables(n, margin)
    places, blocks, at = {}, [], 0
    for name in NAMES:
        block = tables[name]
        places[name] = (at, block.shape[0], block.shape[1])
        blocks.append(np.pad(block, ((0, 0), (0, 2 * n - block.shape[1]))))
        at += block.shape[0]
    return np.concatenate(blocks), places


def split(x):
    high = x.astype(bf16)
    return high, (x - high.astype(f32)).astype(bf16)


def dot(a, b):
    return jnp.dot(a, b, preferred_element_type=f32)


def rows_cat(*parts):
    return jnp.concatenate(parts, axis=0)


def lanes_cat(*parts):
    return jnp.concatenate(parts, axis=1)


def left_wide(table, high, low):
    m = table.shape[0] // 2
    both = dot(table, high)
    return both[:m] + both[m:] + dot(table[:m], low)


def right_wide(x, table):
    m = table.shape[1] // 2
    high, low = split(x)
    both = dot(high, table)
    return both[:, :m] + both[:, m:] + dot(low, table[:, :m])


def sincos_small(r):
    z = r * r
    s = r + r * z * (-1.6666654611e-1 + z * (8.3321608736e-3 + z * -1.9515295891e-4))
    c = 1.0 - 0.5 * z + z * z * (4.166664568298827e-2 + z * (-1.388731625493765e-3 + z * 2.443315711809948e-5))
    return s, c


def quadrant(s, c, q):
    swap = (q & 1) == 1
    sn = jnp.where(swap, c, s)
    cs = jnp.where(swap, s, c)
    sn = jnp.where((q & 2) == 2, -sn, sn)
    cs = jnp.where(((q + 1) & 2) == 2, -cs, cs)
    return sn, cs


def sincos(x, turn):
    k = jnp.round(x * (2.0 / math.pi))
    r = x - k * 1.5703125
    r = r - k * 4.837512969970703125e-4
    r = r - k * 7.549789948768648e-8
    s, c = sincos_small(r)
    return quadrant(s, c, k.astype(jnp.int32) + turn)


def paired(x, r):
    n = x.shape[1] // 2
    return rows_cat(
        lanes_cat(x[:r, :n], x[r:, :n]), lanes_cat(x[:r, n:], x[r:, n:])
    )


def unpaired(x, r):
    n = x.shape[1] // 2
    return rows_cat(
        lanes_cat(x[:r, :n], x[r:, :n]), lanes_cat(x[:r, n:], x[r:, n:])
    )


def forward_pairs(base, pairs, n, modes, coef, chan, zern, mask, t, q_s, f_s, h_s, inv_s):
    side = n // 2
    hr = half_rows(n)
    count = 2 * pairs
    acc = [jnp.zeros((side, n), f32) for _ in range(count)]
    rows = [coef[base + g] for g in range(count)]
    for j in range(modes):
        z = zern[j]
        for g in range(count):
            acc[g] = acc[g] + rows[g][:, j : j + 1] * z
    turn = jnp.where(lax.broadcasted_iota(jnp.int32, (side, n), 1) < side, 1, 0)
    pupils = []
    for g in range(count):
        scale = 1.0 / (1.0 + RATIO * jnp.full((1, n), chan[base + g], jnp.int32).astype(f32))
        sn, cs = sincos(acc[g] * scale, turn)
        pupils.append(mask * sn)
        q_s[base + g] = mask * cs * scale
    for p in range(pairs):
        s0 = base + 2 * p
        high, low = split(rows_cat(pupils[2 * p], pupils[2 * p + 1]))
        half = dot(lanes_cat(high, low), t("t1a")) + dot(high, t("t1l"))
        high, low = split(paired(half, side))
        field = dot(t("t2a"), rows_cat(high, low)) + dot(t("t2l"), high)
        f_s[s0] = field[:, :n]
        f_s[s0 + 1] = field[:, n:]
        inten = field[:n] * field[:n] + field[n:] * field[n:]
        inv0 = 1.0 / jnp.sum(inten[:, :n], keepdims=True)
        inv1 = 1.0 / jnp.sum(inten[:, n:], keepdims=True)
        inv_s[s0] = jnp.broadcast_to(inv0, (8, n))
        inv_s[s0 + 1] = jnp.broadcast_to(inv1, (8, n))
        high, low = split(rows_cat(inten[:, :n], inten[:, n:]))
        inner = dot(lanes_cat(high, low), t("taa")) + dot(high, t("tal"))
        high, low = split(paired(inner, n))
        otf = left_wide(t("tb"), high, low)
        h_s[s0] = otf[:, :n] * inv0
        h_s[s0 + 1] = otf[:, n:] * inv1


def spectrum_pairs(base, pairs, n, pix, shift, chan, t, h_s, s_s, num_s, den_s):
    hr = half_rows(n)
    row = lax.broadcasted_iota(jnp.int32, (hr, n), 0)
    col = lax.broadcasted_iota(jnp.int32, (hr, n), 1)
    num = [[num_s[c, :hr], num_s[c, hr:]] for c in range(CHANNELS)]
    den = [den_s[c] for c in range(CHANNELS)]
    for p in range(pairs):
        s0 = base + 2 * p
        both = rows_cat(pix[s0], pix[s0 + 1])
        inner = dot(lanes_cat(both, both), t("tpa"))
        high, low = split(paired(inner, n))
        spec = left_wide(t("tbp"), high, low)
        for g in range(2):
            s = s0 + g
            sr = spec[:hr, g * n : (g + 1) * n]
            si = spec[hr:, g * n : (g + 1) * n]
            move = shift[s]
            turns = (row * move[:, 0:1] + col * move[:, 1:2]) & (n - 1)
            quarter = n // 4
            q = (turns + quarter // 2) // quarter
            rest = (turns - q * quarter).astype(f32) * (2.0 * math.pi / n)
            sn, cs = quadrant(*sincos_small(rest), q)
            vr = sr * cs - si * sn
            vi = sr * sn + si * cs
            s_s[s, :hr] = vr
            s_s[s, hr:] = vi
            hre = h_s[s, :hr]
            him = h_s[s, hr:]
            cr = hre * vr + him * vi
            ci = hre * vi - him * vr
            power = hre * hre + him * him
            for c in range(CHANNELS):
                mine = jnp.full((1, n), chan[s], jnp.int32) == c
                num[c][0] = num[c][0] + jnp.where(mine, cr, 0.0)
                num[c][1] = num[c][1] + jnp.where(mine, ci, 0.0)
                den[c] = den[c] + jnp.where(mine, power, 0.0)
    for c in range(CHANNELS):
        num_s[c, :hr] = num[c][0]
        num_s[c, hr:] = num[c][1]
        den_s[c] = den[c]


def back_transform(left, right, n, t):
    high, low = split(lanes_cat(left, right))
    part = left_wide(t("ub"), high, low)
    return right_wide(unpaired(part, n), t("ua"))


def backward_pairs(base, pairs, n, modes, chan, zern, t, q_s, f_s, h_s, inv_s, s_s, obj_s, cg_s):
    side = n // 2
    hr = half_rows(n)
    loss = 1.0 / float(n * n * n)
    weights = []
    for p in range(pairs):
        s0 = base + 2 * p
        grads = []
        for g in range(2):
            s = s0 + g
            first = jnp.full((1, n), chan[s], jnp.int32) == 0
            o_re = jnp.where(first, obj_s[0, :hr], obj_s[1, :hr])
            o_im = jnp.where(first, obj_s[0, hr:], obj_s[1, hr:])
            hre = h_s[s, :hr]
            him = h_s[s, hr:]
            rre = s_s[s, :hr] - (o_re * hre - o_im * him)
            rim = s_s[s, hr:] - (o_re * him + o_im * hre)
            grads.append(
                rows_cat(
                    (-2.0 * loss) * (rre * o_re + rim * o_im),
                    (2.0 * loss) * (rre * o_im - rim * o_re),
                )
            )
        psf_grad = back_transform(grads[0], grads[1], n, t)
        field_grads = []
        for g in range(2):
            s = s0 + g
            pg = psf_grad[g * n : (g + 1) * n]
            fr = f_s[s, :n]
            fi = f_s[s, n:]
            inv = inv_s[s][:1]
            mean = inv * jnp.sum(pg * (fr * fr + fi * fi), keepdims=True)
            gi = (2.0 * inv) * (pg - mean)
            field_grads.append(rows_cat(fr * gi, fi * gi))
        high, low = split(lanes_cat(field_grads[0], field_grads[1]))
        part = left_wide(t("u2"), high, low)
        pupil_grad = right_wide(unpaired(part, side), t("u1"))
        for g in range(2):
            weights.append(q_s[s0 + g] * pupil_grad[g * side : (g + 1) * side])
    pad = cg_s.shape[1]
    for j in range(modes):
        z = zern[j]
        for g in range(2 * pairs):
            cg_s[base + g, j : j + 1] = jnp.sum(z * weights[g], axis=0, keepdims=True)


def window_weight(width, n):
    def ramp(axis):
        pos = lax.broadcasted_iota(jnp.int32, (n, n), axis)
        dist = (jnp.minimum(pos, n - 1 - pos) + 1).astype(f32)
        return jnp.minimum(1.0, dist / (jnp.full((1, n), width, jnp.int32).astype(f32) + 1.0))

    return ramp(0) * ramp(1)


def kernel(
    n, modes, slots, group, places, margin,
    chan, inter, coeffs, shifts, mask_ref, pix_in, zern_in, tab_in,
    blended, grad_out,
    q_s, f_s, h_s, inv_s, s_s, num_s, den_s, obj_s, cg_s,
    pix, zern, tab, coef, shift, canvas, strips, landed, part_s, back_s,
    load_sem, c_send, c_recv, s_send, s_recv, p_send, p_recv, m_send, m_recv, g_send, g_recv,
):
    peers = lax.axis_size("patch")
    cols = lax.axis_size("frame")
    me = lax.axis_index("patch")
    col = lax.axis_index("frame")
    local = slots // peers
    hr = half_rows(n)
    pairs = group // 2
    steps = slots // group

    def t(name):
        at, r, c = places[name]
        return tab[at : at + r, :c]

    load_zern = pltpu.make_async_copy(zern_in, zern, load_sem.at[0])
    load_tab = pltpu.make_async_copy(tab_in, tab, load_sem.at[1])
    load_pix = pltpu.make_async_copy(pix_in.at[:, me], pix.at[pl.ds(me * local, local)], load_sem.at[2])
    load_zern.start()
    load_tab.start()
    load_pix.start()

    sides = []
    for dr in (-1, 0, 1):
        for dc in (-1, 0, 1):
            if dr == 0 and dc == 0:
                continue
            strip = {(-1): 0, 1: 1}[dr] if dr else {(-1): 2, 1: 3}[dc]
            place = len(sides)
            sides.append((dr, dc, strip, place))

    def exists(dr, dc):
        ok = (me + dr >= 0) & (me + dr < peers)
        return ok & (col + dc >= 0) & (col + dc < cols)

    landed[...] = jnp.zeros_like(landed)

    barrier = pltpu.get_barrier_semaphore()
    for k in range(1, peers):
        pl.semaphore_signal(
            barrier, inc=1, device_id=(col, lax.rem(me + k, peers)), device_id_type=MESH
        )
    expected = jnp.int32(peers - 1)
    for dr, dc, strip, place in sides:
        if dc == 0:
            continue
        ok = exists(dr, dc)
        expected = expected + jnp.where(ok, 1, 0)

        @pl.when(ok)
        def _():
            pl.semaphore_signal(
                barrier, inc=1, device_id=(col + dc, me + dr), device_id_type=MESH
            )

    cg_s[...] = jnp.zeros_like(cg_s)
    num_s[...] = jnp.zeros_like(num_s)
    den_s[...] = jnp.zeros_like(den_s)
    coef[pl.ds(me * local, local)] = coeffs[:, me]
    shift[pl.ds(me * local, local)] = shifts[:, me]
    m = mask_ref[...].astype(f32)
    mask = lanes_cat(m, m)
    pl.semaphore_wait(barrier, expected)

    def remote(src, dst, send, recv, k, to):
        return pltpu.make_async_remote_copy(
            src_ref=src, dst_ref=dst, send_sem=send.at[k], recv_sem=recv.at[k],
            device_id=to, device_id_type=MESH,
        )

    sends = []
    for k in range(1, peers):
        to = lax.rem(me + k, peers)
        mine = pl.ds(me * local, local)
        device = (col, to)
        sends.append(remote(coeffs.at[:, to], coef.at[mine], c_send, c_recv, k, device))
        sends.append(remote(shifts.at[:, to], shift.at[mine], s_send, s_recv, k, device))
    for k in range(1, peers):
        to = lax.rem(me + k, peers)
        sends.append(
            remote(pix_in.at[:, to], pix.at[pl.ds(me * local, local)], p_send, p_recv, k, (col, to))
        )
    for send in sends:
        send.start()

    def arrived(src, dst, send, recv, k):
        origin = lax.rem(me + peers - k, peers)
        return remote(src.at[:, me], dst.at[pl.ds(origin * local, local)], send, recv, k, (col, origin))

    load_zern.wait()
    load_tab.wait()
    own_first = local % group == 0
    first = me * local // group if own_first else 0

    def wait_coef():
        for k in range(1, peers):
            arrived(coeffs, coef, c_send, c_recv, k).wait_recv()

    if not own_first:
        wait_coef()

    @pl.loop(0, steps)
    def _(i):
        if own_first and peers > 1:
            pl.when(i == local // group)(wait_coef)
        base = lax.rem(first + i, steps) * group
        forward_pairs(base, pairs, n, modes, coef, chan, zern, mask, t, q_s, f_s, h_s, inv_s)

    load_pix.wait()
    for k in range(1, peers):
        arrived(shifts, shift, s_send, s_recv, k).wait_recv()
        arrived(pix_in, pix, p_send, p_recv, k).wait_recv()

    @pl.loop(0, steps)
    def _(i):
        spectrum_pairs(i * group, pairs, n, pix, shift, chan, t, h_s, s_s, num_s, den_s)

    for c in range(CHANNELS):
        d = 1.0 / (den_s[c] + GAMMA)
        obj_s[c, :hr] = num_s[c, :hr] * d
        obj_s[c, hr:] = num_s[c, hr:] * d
    images = back_transform(obj_s[0], obj_s[1], n, t) * (1.0 / (n * n))
    weight = window_weight(inter[0, 0], n)
    layers = (images[:n] * weight, images[n:] * weight, weight)
    for c, layer in enumerate(layers):
        canvas[c] = layer
        turned = layer.T
        strips[0, c] = layer[:margin]
        strips[1, c] = layer[n - margin :]
        strips[2, c] = turned[:margin]
        strips[3, c] = turned[n - margin :]

    def margin_copy(dr, dc, strip, place):
        there = len(sides) - 1 - place
        return pltpu.make_async_remote_copy(
            src_ref=strips.at[strip], dst_ref=landed.at[there],
            send_sem=m_send.at[place], recv_sem=m_recv.at[there],
            device_id=(col + dc, me + dr), device_id_type=MESH,
        )

    def margin_landed(dr, dc, strip, place):
        return pltpu.make_async_remote_copy(
            src_ref=strips.at[strip], dst_ref=landed.at[place],
            send_sem=m_send.at[place], recv_sem=m_recv.at[place],
            device_id=(col + dc, me + dr), device_id_type=MESH,
        )

    for side in sides:
        @pl.when(exists(side[0], side[1]))
        def _():
            margin_copy(*side).start()

    @pl.loop(0, steps)
    def _(i):
        backward_pairs(
            i * group, pairs, n, modes, chan, zern, t, q_s, f_s, h_s, inv_s, s_s, obj_s, cg_s
        )

    pad = cg_s.shape[1]
    flat = cg_s[...].reshape(slots * pad, n)
    sums = lax.dot_general(
        jnp.ones((8, n), f32), flat, (((1,), (1,)), ((), ())),
        precision=lax.Precision.HIGHEST, preferred_element_type=f32,
    )
    for s in range(slots):
        part_s[s] = sums[0:1, s * pad : s * pad + modes]
    back = []
    for k in range(1, peers):
        to = lax.rem(me + k, peers)
        back.append(
            remote(part_s.at[pl.ds(to * local, local)], back_s.at[:, me], g_send, g_recv, k, (col, to))
        )
    for send in back:
        send.start()
    back_s[:, me] = part_s[pl.ds(me * local, local)]

    for side in sides:
        @pl.when(exists(side[0], side[1]))
        def _():
            margin_landed(*side).wait_recv()

    where = {(dr, dc): place for dr, dc, strip, place in sides}
    lane = lax.broadcasted_iota(jnp.int32, (margin, n), 1)
    near = (lane >= margin) & (lane < 2 * margin)
    far = (lane >= n - 2 * margin) & (lane < n - margin)
    gap = jnp.zeros((margin, n), f32)
    wide = jnp.zeros((n - 4 * margin, n), f32)
    folded = []
    for c in range(CHANNELS + 1):
        def edge(dr):
            corner_l = pltpu.roll(landed[where[dr, -1], c], 2 * margin, 1)
            corner_r = pltpu.roll(landed[where[dr, 1], c], n - 2 * margin, 1)
            return (
                landed[where[dr, 0], c]
                + jnp.where(near, corner_l, 0.0)
                + jnp.where(far, corner_r, 0.0)
            )

        turned = rows_cat(gap, landed[where[0, -1], c], wide, landed[where[0, 1], c], gap)
        rows = rows_cat(gap, edge(-1), wide, edge(1), gap)
        folded.append(canvas[c] + turned.T + rows)
    inverse = 1.0 / folded[CHANNELS][margin : n - margin, margin : n - margin]
    for c in range(CHANNELS):
        blended[c] = folded[c][margin : n - margin, margin : n - margin] * inverse

    for k in range(1, peers):
        origin = lax.rem(me + peers - k, peers)
        remote(
            part_s.at[pl.ds(me * local, local)], back_s.at[:, origin], g_send, g_recv, k, (col, origin)
        ).wait_recv()
    grad_out[...] = back_s[...]
    for send in sends + back:
        send.wait_send()
    for side in sides:
        @pl.when(exists(side[0], side[1]))
        def _():
            margin_copy(*side).wait_send()


def per_device(coeffs, shifts, pixels, pupil_mask, chan_map, intersection):
    local, rows, _, modes = coeffs.shape
    n = pixels.shape[3]
    margin = MARGIN
    slots = chan_map.shape[0]
    group = 4
    hr = half_rows(n)
    side = n // 2
    pad = -(-modes // 8) * 8
    peers = lax.axis_size("patch")
    z = zernike_basis(modes, side)
    zern = np.concatenate([z, z], axis=2).astype(np.float32)
    tables, places = pack_tables(n, margin)
    tile = n - 2 * margin
    smem = pl.BlockSpec(memory_space=pltpu.SMEM)
    vmem = pl.BlockSpec(memory_space=pltpu.VMEM)
    anywhere = pl.BlockSpec(memory_space=pl.ANY)
    dma = pltpu.SemaphoreType.DMA
    blended, grad = pl.pallas_call(
        functools.partial(kernel, n, modes, slots, group, places, margin),
        out_shape=(
            jax.ShapeDtypeStruct((CHANNELS, tile, tile), f32),
            jax.ShapeDtypeStruct((local, rows, 1, modes), f32),
        ),
        in_specs=[smem] * 2 + [vmem] * 3 + [anywhere] * 3,
        out_specs=(vmem, vmem),
        scratch_shapes=[
            pltpu.VMEM((slots, side, n), f32),
            pltpu.VMEM((slots, 2 * n, n), f32),
            pltpu.VMEM((slots, 2 * hr, n), f32),
            pltpu.VMEM((slots, 8, n), f32),
            pltpu.VMEM((slots, 2 * hr, n), f32),
            pltpu.VMEM((CHANNELS, 2 * hr, n), f32),
            pltpu.VMEM((CHANNELS, hr, n), f32),
            pltpu.VMEM((CHANNELS, 2 * hr, n), f32),
            pltpu.VMEM((slots, pad, n), f32),
            pltpu.VMEM((slots, n, n), bf16),
            pltpu.VMEM(zern.shape, f32),
            pltpu.VMEM(tables.shape, bf16),
            pltpu.VMEM((slots, 1, modes), f32),
            pltpu.VMEM((slots, 1, 2), jnp.int32),
            pltpu.VMEM((CHANNELS + 1, n, n), f32),
            pltpu.VMEM((4, CHANNELS + 1, margin, n), f32),
            pltpu.VMEM((8, CHANNELS + 1, margin, n), f32),
            pltpu.VMEM((slots, 1, modes), f32),
            pltpu.VMEM((local, rows, 1, modes), f32),
            dma((3,)),
        ]
        + [dma((peers,))] * 6
        + [dma((8,))] * 2
        + [dma((peers,))] * 2,
        compiler_params=pltpu.CompilerParams(
            vmem_limit_bytes=48 * 1024 * 1024, collective_id=0, has_side_effects=True
        ),
    )(
        chan_map, intersection, coeffs, shifts, pupil_mask,
        pixels.reshape(local, rows, n, n), jnp.asarray(zern), jnp.asarray(tables),
    )
    return (blended, grad)


def solution(mesh):
    in_specs = (
        P("patch", None, "frame", None),
        P("patch", None, "frame", None),
        P("patch", None, "frame", None, None),
        P(),
        P(),
        P("patch", "frame"),
    )
    out_specs = (P(None, "patch", "frame"), P("patch", None, "frame", None))
    return jax.shard_map(
        per_device, mesh=mesh, in_specs=in_specs, out_specs=out_specs, check_vma=False
    )
```
